32 devices in a mesh: tm: 2 (over x), tile: 16 (over z, y, core).
Axes of the slice: x: 2, y: 2, z: 4, core: 2. Of those that a mesh axis runs over, the one named last changes fastest.
Arguments:
- starts: float32 [2, 24576, 128], P('tm', 'tile'), may hold values from -6 to 6
- sources: float32 [24576, 128], P('tile'), may hold values from -6 to 6
- fine_ops: float32 [2, 192, 4, 128, 128], P('tm', 'tile'), may hold values from -0.1875 to 0.1875
- col_index: int32 [2, 192, 4], P('tm', 'tile'), may hold values from 0 to 15, as said below
- live_count: int32 [2, 192], P('tm', 'tile'), may hold values from 1 to 4, as said below
- coarse_op: float32 [6144, 768], P('tile'), may hold values from -0.15625 to 0.15625
- cell_map: int32 [24576], P('tile'), may hold values from 0 to 383, as said below
Outputs:
- corrected: float32 [2, 24576, 128], P('tm', 'tile')
The draws below stay inside these ranges and needn't reach their ends.
Inputs may be any that keep to these rules, and one draw needn't show every extreme that they name: `col_index`: each entry names one of the 16 blocks of a tile's fine window. Slots from live_count on are padding and carry no transport. `cell_map`: each entry is a local coarse index within its own tile; every coarse cell of every tile has at least one fine cell.
All inputs are finite; a program needn't handle non-finite values.
Results may differ from the reference program's by a relative error of at most 0.0003.
Values sent between devices are 32-bit elements; how exact they have to be, the bound alone decides.
A program may use at most 64 MiB of HBM per device.

```python
import jax
import jax.numpy as jnp
from jax import lax

NTR = 128
BS = 128
ROWS = 1536
HALO = 256
KMAX = 4
STEPS = 2
SLICES = 2
CELLS = 24576
COARSE = 384
CHALO = 192


def draw_col_index(key, part):
    tile_count = CELLS // ROWS
    block_count = ROWS // BS
    window = (ROWS + 2 * HALO) // BS
    key_cols = jax.random.fold_in(key, 11)
    key_pick = jax.random.fold_in(key, 12)
    columns = jax.random.randint(key_cols, (SLICES, tile_count, block_count, KMAX), 0, window)
    chosen = jax.random.randint(key_pick, (SLICES, tile_count, 1, 1), 0, block_count)
    block_ids = jnp.arange(block_count)[None, None, :, None]
    slot_ids = jnp.arange(KMAX)[None, None, None, :]
    columns = jnp.where((block_ids == chosen) & (slot_ids == 0), window - 1, columns)
    columns = jnp.where((block_ids == chosen) & (slot_ids == 1), 0, columns)
    return columns.reshape(SLICES, CELLS // BS, KMAX).astype(jnp.int32)


def draw_live_count(key, part):
    tile_count = CELLS // ROWS
    block_count = ROWS // BS
    key_cap = jax.random.fold_in(key, 21)
    key_top = jax.random.fold_in(key, 22)
    key_fill = jax.random.fold_in(key, 23)
    key_pick = jax.random.fold_in(key, 24)
    key_low = jax.random.fold_in(key, 25)
    ceilings = jax.random.randint(key_cap, (SLICES, tile_count), 2, KMAX + 1)
    busiest = jax.random.randint(key_top, (SLICES, 1), 0, tile_count)
    ceilings = jnp.where(jnp.arange(tile_count)[None, :] == busiest, KMAX, ceilings)
    counted = jax.random.randint(key_fill, (SLICES, tile_count, block_count), 1, ceilings[:, :, None] + 1)
    chosen = jax.random.randint(key_pick, (SLICES, tile_count, 1), 0, block_count)
    lowest = (chosen + 1 + jax.random.randint(key_low, (SLICES, tile_count, 1), 0, block_count - 1)) % block_count
    block_ids = jnp.arange(block_count)[None, None, :]
    counted = jnp.where(block_ids == chosen, ceilings[:, :, None], counted)
    counted = jnp.where(block_ids == lowest, 1, counted)
    return counted.reshape(SLICES, CELLS // BS).astype(jnp.int32)


def draw_cell_map(key, part):
    tile_count = CELLS // ROWS
    key_map = jax.random.fold_in(key, 31)
    key_perm = jax.random.fold_in(key, 32)
    mapping = jax.random.randint(key_map, (tile_count, ROWS), 0, COARSE)
    orders = jax.vmap(lambda sub_key: jax.random.permutation(sub_key, ROWS))(jax.random.split(key_perm, tile_count))
    mapping = mapping.at[jnp.arange(tile_count)[:, None], orders[:, :COARSE]].set(jnp.arange(COARSE, dtype=jnp.int32)[None, :])
    return mapping.reshape(CELLS).astype(jnp.int32)


def shard_levels(stream_key, extent, cuts, smallest, top_value):
    level, own = 1.0, jax.random.fold_in(stream_key, 6)
    for position, shards_of in cuts:
        heights = jnp.exp(jax.random.uniform(jax.random.fold_in(own, position), (shards_of,), jnp.float32, smallest / len(cuts), top_value / len(cuts)))
        level = level * jnp.repeat(heights, extent[position] // shards_of).reshape([-1 if axis == position else 1 for axis in range(len(extent))])
    return level


def centred(stream_key, extent, scale, limit, cuts=(), held_as=jnp.bfloat16):
    values = scale * jax.random.normal(stream_key, extent, jnp.float32)
    if cuts:
        values = values * shard_levels(stream_key, extent, cuts, -0.22, 0.18)
    return jnp.clip(values, -limit, limit).astype(held_as)


def setup_inputs(seed: int = 0) -> dict:
    arg_keys = jax.random.split(jax.random.key(seed), 8)
    return {
        "starts": centred(arg_keys[0], (SLICES, CELLS, NTR), 1.0, 6.0, ((0, 2), (1, 16)), jnp.float32),
        "sources": centred(arg_keys[1], (CELLS, NTR), 1.0, 6.0, ((0, 16),), jnp.float32),
        "fine_ops": centred(arg_keys[2], (SLICES, CELLS // BS, KMAX, BS, BS), (2 * KMAX * BS) ** -0.5, 0.1875, ((0, 2), (1, 16)), jnp.float32),
        "col_index": draw_col_index(jax.random.fold_in(arg_keys[7], 71), 0),
        "live_count": draw_live_count(jax.random.fold_in(arg_keys[7], 71), 0),
        "coarse_op": centred(arg_keys[5], (CELLS // 4, COARSE + 2 * CHALO), (2 * (COARSE + 2 * CHALO)) ** -0.5, 0.15625, ((0, 16),), jnp.float32),
        "cell_map": draw_cell_map(jax.random.fold_in(arg_keys[7], 71), 0),
    }


def extend(tiled, width):
    lower_rim = jnp.roll(tiled, 1, axis=0)[:, tiled.shape[1] - width:]
    upper_rim = jnp.roll(tiled, -1, axis=0)[:, :width]
    return jnp.concatenate([lower_rim, tiled, upper_rim], axis=1)


def fine_step(tracer_state, sources, transport, columns, slot_counts):
    tile_count = CELLS // ROWS
    block_count = ROWS // BS
    extended = extend(tracer_state.reshape(tile_count, ROWS, NTR), HALO)
    extended = extended.reshape(tile_count, (ROWS + 2 * HALO) // BS, BS, NTR)

    def one_tile(packed):
        ext_blocks, block_ops, block_cols, block_counts = packed
        live_mask = (jnp.arange(KMAX)[None, :] < block_counts[:, None]).astype(jnp.float32)
        pieces = ext_blocks[block_cols] * live_mask[:, :, None, None]
        return jnp.einsum("bkij,bkjn->bin", block_ops, pieces, precision=lax.Precision.HIGHEST)

    transported = lax.map(one_tile, (extended,
                                     transport.reshape(tile_count, block_count, KMAX, BS, BS),
                                     columns.reshape(tile_count, block_count, KMAX),
                                     slot_counts.reshape(tile_count, block_count)))
    return transported.reshape(CELLS, NTR) + sources


def coarse_apply(coarse_state, coarse_op):
    tile_count = CELLS // ROWS
    extended = extend(coarse_state.reshape(tile_count, COARSE, NTR), CHALO)
    operator = coarse_op.reshape(tile_count, COARSE, COARSE + 2 * CHALO)
    result = jnp.einsum("tcj,tjn->tcn", operator, extended, precision=lax.Precision.HIGHEST)
    return result.reshape(tile_count * COARSE, NTR)


def reference(starts, sources, fine_ops, col_index, live_count, coarse_op, cell_map):
    tile_count = CELLS // ROWS
    tiled_map = cell_map.reshape(tile_count, ROWS)
    onehot = (tiled_map[:, :, None] == jnp.arange(COARSE, dtype=jnp.int32)[None, None, :]).astype(jnp.float32)
    children = jnp.sum(onehot, axis=1)

    def restrict(values_in):
        sums = jnp.einsum("tic,tin->tcn", onehot, values_in.reshape(tile_count, ROWS, NTR),
                          precision=lax.Precision.HIGHEST)
        return (sums / children[:, :, None]).reshape(tile_count * COARSE, NTR)

    def prolong(coarse_values):
        spread = jnp.einsum("tic,tcn->tin", onehot, coarse_values.reshape(tile_count, COARSE, NTR),
                            precision=lax.Precision.HIGHEST)
        return spread.reshape(CELLS, NTR)

    fine_ends = []
    for slice_index in range(SLICES):
        tracer_state = starts[slice_index]
        for step_index in range(STEPS):
            tracer_state = fine_step(tracer_state, sources, fine_ops[slice_index],
                                     col_index[slice_index], live_count[slice_index])
        fine_ends.append(tracer_state)
    coarse_state = jnp.zeros((tile_count * COARSE, NTR), jnp.float32)
    outputs = []
    for slice_index in range(SLICES):
        if slice_index + 1 < SLICES:
            following = starts[slice_index + 1]
        else:
            following = jnp.zeros((CELLS, NTR), jnp.float32)
        jump_term = restrict(fine_ends[slice_index] - following)
        coarse_image = coarse_apply(coarse_state, coarse_op)
        outputs.append(fine_ends[slice_index] + prolong(coarse_image))
        coarse_state = coarse_image + jump_term
    return jnp.stack(outputs)
```

```python
import jax
import jax.numpy as jnp
from jax import lax
from jax.experimental import pallas as pl
from jax.experimental.pallas import tpu as pltpu
from jax.sharding import PartitionSpec as P

MESH = pl.DeviceIdType.MESH
HALO = 256
STEPS = 2
F32, BF16 = jnp.float32, jnp.bfloat16


def parts(x):
    high = x.astype(BF16)
    return high, (x - high.astype(F32)).astype(BF16)


def beside(x):
    return jnp.concatenate(parts(x), axis=1)


def dot(a, b):
    return jnp.dot(a, b, preferred_element_type=F32)


def kernel(
    starts, sources, ops, coarse_op, map_ref, cols, live, out,
    start_v, source_v, ops_v, coarse_v, ops_2, coarse_2, win, edge, halo,
    gather_m, spread_m, inverse, fine, fine_2, following, follow_src, jump, sent, state, image, result,
    load_sem, ops_sem, halo_send, halo_recv, tm_send, tm_recv, out_sem,
):
    tm, tile = lax.axis_index("tm"), lax.axis_index("tile")
    slices, tiles = lax.axis_size("tm"), lax.axis_size("tile")
    right, left = lax.rem(tile + 1, tiles), lax.rem(tile + tiles - 1, tiles)
    rows, tracers = starts.shape
    blocks, slots, size, _ = ops.shape
    coarse = coarse_op.shape[0]
    rim = state.shape[1]
    rim_blocks = HALO // size
    first, last = tm == 0, tm == slices - 1

    loads = [
        pltpu.make_async_copy(starts, start_v, load_sem.at[0]),
        pltpu.make_async_copy(sources, source_v, load_sem.at[1]),
        pltpu.make_async_copy(coarse_op, coarse_v, load_sem.at[2]),
    ]
    loads[0].start()

    def ops_load(b):
        return pltpu.make_async_copy(ops.at[b], ops_v.at[b], ops_sem.at[b])

    barrier = pltpu.get_barrier_semaphore()
    for other in (left, right):
        pl.semaphore_signal(barrier, inc=1, device_id=(tm, other), device_id_type=MESH)

    @pl.when(tm > 0)
    def _():
        pl.semaphore_signal(barrier, inc=1, device_id=(tm - 1, tile), device_id_type=MESH)

    @pl.when(tm < slices - 1)
    def _():
        pl.semaphore_signal(barrier, inc=1, device_id=(tm + 1, tile), device_id_type=MESH)

    @pl.loop(0, blocks)
    def _(b):
        ops_load(b).start()

    loads[1].start()
    loads[2].start()
    expected = 2 + jnp.where(first, 0, 1) + jnp.where(last, 0, 1)
    pl.semaphore_wait(barrier, expected)

    def halo_copies(step):
        if step == 0:
            head, tail = starts.at[pl.ds(0, HALO)], starts.at[pl.ds(rows - HALO, HALO)]
        else:
            head, tail = edge.at[step - 1, 0], edge.at[step - 1, 1]
        return [
            pltpu.make_async_remote_copy(
                src_ref=src, dst_ref=halo.at[step, side], send_sem=halo_send.at[step, side],
                recv_sem=halo_recv.at[step, side], device_id=(tm, to), device_id_type=MESH,
            )
            for side, src, to in ((0, tail, right), (1, head, left))
        ]

    exchanges = [halo_copies(step) for step in range(STEPS)]
    for copy in exchanges[0]:
        copy.start()

    hits = lax.broadcasted_iota(jnp.int32, (coarse, rows), 0) == map_ref[...]
    ones = jnp.where(hits, 1.0, 0.0)
    gather_m[...] = ones.astype(BF16)
    inverse[...] = jnp.broadcast_to(1.0 / jnp.sum(ones, axis=1, keepdims=True), (coarse, tracers))

    def restricted(low, high):
        both = dot(gather_m[low:high, :], fine_2[...])
        return (both[:, :tracers] + both[:, tracers:]) * inverse[low:high, :]

    loads[0].wait()

    @pl.loop(0, blocks)
    def _(b):
        here = pl.ds(pl.multiple_of(b * size, size), size)
        pair = beside(start_v[here, :])
        win[0, b + rim_blocks] = pair
        fine_2[here, :] = pair

    following_copy = pltpu.make_async_remote_copy(
        src_ref=follow_src, dst_ref=following, send_sem=tm_send.at[0], recv_sem=tm_recv.at[0],
        device_id=(lax.max(tm - 1, 0), tile), device_id_type=MESH,
    )
    follow_src[...] = restricted(0, coarse)

    @pl.when(tm > 0)
    def _():
        following_copy.start()

    @pl.loop(0, blocks)
    def _(b):
        ops_load(b).wait()
        for k in range(slots):
            kept = jnp.where(k < live[0, b], 1.0, 0.0)
            high, low = parts(ops_v[b, k] * kept)
            ops_2[b, 0:size, k * size:(k + 1) * size] = high
            ops_2[b, size:2 * size, k * size:(k + 1) * size] = low

    loads[1].wait()

    def take_halo(step):
        for side, copy in enumerate(exchanges[step]):
            copy.wait_recv()
            at = 0 if side == 0 else rim_blocks + blocks
            for i in range(rim_blocks):
                win[step, at + i] = beside(halo[step, side, i * size:(i + 1) * size, :])

    def row_block(step, b):
        pieces = jnp.concatenate([win[step, cols[k, b]] for k in range(slots)], axis=0)
        four = dot(ops_2[b], pieces)
        moved = four[:size, :tracers] + (four[:size, tracers:] + four[size:, :tracers])
        return moved + source_v[pl.ds(pl.multiple_of(b * size, size), size), :]

    def coarse_image():
        held = beside(state[...].reshape(4 * rim, tracers))
        four = dot(coarse_2[...], held)
        image[...] = four[:coarse, :tracers] + (four[:coarse, tracers:] + four[coarse:, :tracers])

    loads[2].wait()
    high, low = parts(coarse_v[...])
    coarse_2[0:coarse, :] = high
    coarse_2[coarse:, :] = low

    @pl.when(first)
    def _():
        state[...] = jnp.zeros(state.shape, F32)
        coarse_image()

    @pl.when(last)
    def _():
        following[...] = jnp.zeros(following.shape, F32)

    for step in range(STEPS - 1):
        take_halo(step)

        def edge_block(side, i):
            b = i if side == 0 else blocks - rim_blocks + i
            new = row_block(step, b)
            edge[step, side, i * size:(i + 1) * size, :] = new
            win[step + 1, b + rim_blocks] = beside(new)

        for side in (0, 1):
            for i in range(rim_blocks):
                edge_block(side, i)
            exchanges[step + 1][1 - side].start()

        @pl.loop(rim_blocks, blocks - rim_blocks)
        def _(b):
            win[step + 1, b + rim_blocks] = beside(row_block(step, b))

    @pl.loop(0, rows // size)
    def _(j):
        here = pl.ds(pl.multiple_of(j * size, size), size)
        lane = jnp.broadcast_to(map_ref[:, here].astype(F32), (size, size))
        column = jnp.transpose(lane).astype(jnp.int32)
        for g in range(coarse // size):
            want = lax.broadcasted_iota(jnp.int32, (size, size), 1) + g * size
            spread_m[here, g * size:(g + 1) * size] = jnp.where(column == want, 1.0, 0.0).astype(BF16)

    take_halo(STEPS - 1)

    @pl.loop(0, blocks)
    def _(b):
        new = row_block(STEPS - 1, b)
        here = pl.ds(pl.multiple_of(b * size, size), size)
        fine[here, :] = new
        fine_2[here, :] = beside(new)

    @pl.when(tm < slices - 1)
    def _():
        following_copy.wait_recv()

    following_tile = lax.min(tm + 1, slices - 1)
    state_copies = [
        pltpu.make_async_remote_copy(
            src_ref=sent.at[half], dst_ref=state.at[1 + half], send_sem=tm_send.at[1 + half],
            recv_sem=tm_recv.at[1 + half], device_id=(following_tile, tile), device_id_type=MESH,
        )
        for half in range(2)
    ]
    rim_copies = [
        pltpu.make_async_remote_copy(
            src_ref=state.at[1 + half], dst_ref=state.at[3 if half == 0 else 0], send_sem=tm_send.at[3 + half],
            recv_sem=tm_recv.at[3 + half], device_id=(tm, left if half == 0 else right), device_id_type=MESH,
        )
        for half in range(2)
    ]
    for half in (1, 0):
        span = slice(half * rim, (half + 1) * rim)
        jump[span, :] = restricted(half * rim, (half + 1) * rim) - following[span, :]

        @pl.when(first)
        def _():
            sent[half] = image[span, :] + jump[span, :]
            state_copies[half].start()

    @pl.when(tm > 0)
    def _():
        for half in (1, 0):
            state_copies[half].wait_recv()
            rim_copies[half].start()
        for half in (1, 0):
            rim_copies[half].wait_recv()
        coarse_image()

        @pl.when(tm < slices - 1)
        def _():
            for half in (1, 0):
                span = slice(half * rim, (half + 1) * rim)
                sent[half] = image[span, :] + jump[span, :]
                state_copies[half].start()

    pair = beside(image[...])
    pieces = out_sem.shape[0]
    some = rows // pieces
    stores = []
    for i in range(pieces):
        span = slice(i * some, (i + 1) * some)
        both = dot(spread_m[span, :], pair)
        result[span, :] = fine[span, :] + (both[:, :tracers] + both[:, tracers:])
        stores.append(pltpu.make_async_copy(result.at[pl.ds(i * some, some)], out.at[pl.ds(i * some, some)], out_sem.at[i]))
        stores[-1].start()

    for exchange in exchanges:
        for copy in exchange:
            copy.wait_send()

    @pl.when(tm > 0)
    def _():
        following_copy.wait_send()
        for copy in rim_copies:
            copy.wait_send()

    @pl.when(tm < slices - 1)
    def _():
        for copy in state_copies:
            copy.wait_send()

    for store in stores:
        store.wait()


def on_device(starts, sources, fine_ops, col_index, live_count, coarse_op, cell_map):
    rows, tracers = sources.shape
    _, blocks, slots, size, _ = fine_ops.shape
    coarse, wide = coarse_op.shape
    rim = (wide - coarse) // 2
    window = blocks + 2 * HALO // size
    anywhere = pl.BlockSpec(memory_space=pl.ANY)
    vmem = pl.BlockSpec(memory_space=pltpu.VMEM)
    smem = pl.BlockSpec(memory_space=pltpu.SMEM)
    dma = pltpu.SemaphoreType.DMA
    pieces = 4
    result = pl.pallas_call(
        kernel,
        out_shape=jax.ShapeDtypeStruct((rows, tracers), F32),
        in_specs=[anywhere, anywhere, anywhere, anywhere, vmem, smem, smem],
        out_specs=anywhere,
        scratch_shapes=[
            pltpu.VMEM((rows, tracers), F32),
            pltpu.VMEM((rows, tracers), F32),
            pltpu.VMEM((blocks, slots, size, size), F32),
            pltpu.VMEM((coarse, wide), F32),
            pltpu.VMEM((blocks, 2 * size, slots * size), BF16),
            pltpu.VMEM((2 * coarse, wide), BF16),
            pltpu.VMEM((STEPS, window, size, 2 * tracers), BF16),
            pltpu.VMEM((STEPS - 1, 2, HALO, tracers), F32),
            pltpu.VMEM((STEPS, 2, HALO, tracers), F32),
            pltpu.VMEM((coarse, rows), BF16),
            pltpu.VMEM((rows, coarse), BF16),
            pltpu.VMEM((coarse, tracers), F32),
            pltpu.VMEM((rows, tracers), F32),
            pltpu.VMEM((rows, 2 * tracers), BF16),
            pltpu.VMEM((coarse, tracers), F32),
            pltpu.VMEM((coarse, tracers), F32),
            pltpu.VMEM((coarse, tracers), F32),
            pltpu.VMEM((2, rim, tracers), F32),
            pltpu.VMEM((4, rim, tracers), F32),
            pltpu.VMEM((coarse, tracers), F32),
            pltpu.VMEM((rows, tracers), F32),
            dma((3,)),
            dma((blocks,)),
            dma((STEPS, 2)),
            dma((STEPS, 2)),
            dma((5,)),
            dma((5,)),
            dma((pieces,)),
        ],
        compiler_params=pltpu.CompilerParams(
            collective_id=0, has_side_effects=True, vmem_limit_bytes=48 * 2**20
        ),
    )(
        starts[0], sources, fine_ops[0], coarse_op, cell_map.reshape(1, rows), col_index[0].T, live_count,
    )
    return result[None]


def solution(mesh):
    placed = (
        P("tm", "tile", None),
        P("tile", None),
        P("tm", "tile", None, None, None),
        P("tm", "tile", None),
        P("tm", "tile"),
        P("tile", None),
        P("tile"),
    )
    return jax.shard_map(
        on_device, mesh=mesh, in_specs=placed, out_specs=P("tm", "tile", None), check_vma=False
    )
```

```python
import jax
import jax.numpy as jnp
from jax import lax
from jax.experimental import pallas as pl
from jax.experimental.pallas import tpu as pltpu
from jax.sharding import PartitionSpec as P

MESH = pl.DeviceIdType.MESH
HALO = 256
STEPS = 2
CHUNKS = 4
F32, BF16 = jnp.float32, jnp.bfloat16


def parts(x):
    high = x.astype(BF16)
    return high, (x - high.astype(F32)).astype(BF16)


def beside(x):
    return jnp.concatenate(parts(x), axis=1)


def dot(a, b):
    return jnp.dot(a, b, preferred_element_type=F32)


def kernel(
    starts, sources, ops, coarse_op, map_hbm, cols_hbm, live_hbm, out,
    map_v, cols, live, start_v, source_v, ops_v, coarse_v, ops_2, coarse_own, coarse_rims, win, edge, halo,
    gather_m, spread_m, inverse, fine, fine_2, following, follow_src, jump, sent, state, image,
    load_sem, ops_sem, halo_send, halo_recv, tm_send, tm_recv,
):
    tm, tile = lax.axis_index("tm"), lax.axis_index("tile")
    slices, tiles = lax.axis_size("tm"), lax.axis_size("tile")
    right, left = lax.rem(tile + 1, tiles), lax.rem(tile + tiles - 1, tiles)
    rows, tracers = starts.shape
    blocks, slots, size, _ = ops.shape
    coarse = coarse_op.shape[0]
    rim = state.shape[1]
    rim_blocks = HALO // size
    first, last = tm == 0, tm == slices - 1

    loads = [
        pltpu.make_async_copy(starts, start_v, load_sem.at[0]),
        pltpu.make_async_copy(sources, source_v, load_sem.at[1]),
        pltpu.make_async_copy(coarse_op, coarse_v, load_sem.at[2]),
        pltpu.make_async_copy(live_hbm, live, load_sem.at[3]),
        pltpu.make_async_copy(cols_hbm, cols, load_sem.at[4]),
        pltpu.make_async_copy(map_hbm, map_v, load_sem.at[5]),
    ]
    for at in (0, 3, 4, 5):
        loads[at].start()

    def ops_load(b):
        return pltpu.make_async_copy(ops.at[b], ops_v.at[b], ops_sem.at[b])

    barrier = pltpu.get_barrier_semaphore()
    for other in (left, right):
        pl.semaphore_signal(barrier, inc=1, device_id=(tm, other), device_id_type=MESH)

    @pl.when(tm > 0)
    def _():
        pl.semaphore_signal(barrier, inc=1, device_id=(tm - 1, tile), device_id_type=MESH)

    @pl.when(tm < slices - 1)
    def _():
        pl.semaphore_signal(barrier, inc=1, device_id=(tm + 1, tile), device_id_type=MESH)

    @pl.loop(0, blocks)
    def _(b):
        ops_load(b).start()

    loads[1].start()
    loads[2].start()
    expected = 2 + jnp.where(first, 0, 1) + jnp.where(last, 0, 1)
    pl.semaphore_wait(barrier, expected)

    def halo_copies(step):
        if step == 0:
            head, tail = starts.at[pl.ds(0, HALO)], starts.at[pl.ds(rows - HALO, HALO)]
        else:
            head, tail = edge.at[step - 1, 0], edge.at[step - 1, 1]
        return [
            pltpu.make_async_remote_copy(
                src_ref=src, dst_ref=halo.at[step, side], send_sem=halo_send.at[step, side],
                recv_sem=halo_recv.at[step, side], device_id=(tm, to), device_id_type=MESH,
            )
            for side, src, to in ((0, tail, right), (1, head, left))
        ]

    exchanges = [halo_copies(step) for step in range(STEPS)]
    for copy in exchanges[0]:
        copy.start()

    def restricted(low, high):
        both = dot(gather_m[low:high, :], fine_2[...])
        return (both[:, :tracers] + both[:, tracers:]) * inverse[low:high, :]

    loads[0].wait()

    @pl.loop(0, blocks)
    def _(b):
        here = pl.ds(pl.multiple_of(b * size, size), size)
        pair = beside(start_v[here, :])
        win[0, b + rim_blocks] = pair
        fine_2[here, :] = pair

    loads[3].wait()

    @pl.loop(0, blocks)
    def _(b):
        ops_load(b).wait()
        for k in range(slots):
            kept = jnp.where(k < live[0, b], 1.0, 0.0)
            high, low = parts(ops_v[b, k] * kept)
            ops_2[b, 0:size, k * size:(k + 1) * size] = high
            ops_2[b, size:2 * size, k * size:(k + 1) * size] = low

    loads[1].wait()
    loads[4].wait()
    loads[5].wait()

    def take_halo(step):
        for side, copy in enumerate(exchanges[step]):
            copy.wait_recv()
            at = 0 if side == 0 else rim_blocks + blocks
            for i in range(rim_blocks):
                win[step, at + i] = beside(halo[step, side, i * size:(i + 1) * size, :])

    def row_block(step, b):
        pieces = jnp.concatenate([win[step, cols[k, b]] for k in range(slots)], axis=0)
        four = dot(ops_2[b], pieces)
        moved = four[:size, :tracers] + (four[:size, tracers:] + four[size:, :tracers])
        return moved + source_v[pl.ds(pl.multiple_of(b * size, size), size), :]

    def coarse_part(operator, low, high):
        held = beside(jnp.concatenate([state[low], state[high]], axis=0))
        four = dot(operator[...], held)
        return four[:coarse, :tracers] + (four[:coarse, tracers:] + four[coarse:, :tracers])

    hits = lax.broadcasted_iota(jnp.int32, (coarse, rows), 0) == map_v[...].reshape(1, rows)
    ones = jnp.where(hits, 1.0, 0.0)
    gather_m[...] = ones.astype(BF16)
    inverse[...] = jnp.broadcast_to(1.0 / jnp.sum(ones, axis=1, keepdims=True), (coarse, tracers))

    for step in range(STEPS - 1):
        take_halo(step)

        def edge_block(side, i):
            b = i if side == 0 else blocks - rim_blocks + i
            new = row_block(step, b)
            edge[step, side, i * size:(i + 1) * size, :] = new
            win[step + 1, b + rim_blocks] = beside(new)

        for side in (0, 1):
            for i in range(rim_blocks):
                edge_block(side, i)
            exchanges[step + 1][1 - side].start()

        @pl.loop(rim_blocks, blocks - rim_blocks)
        def _(b):
            win[step + 1, b + rim_blocks] = beside(row_block(step, b))

    following_copy = pltpu.make_async_remote_copy(
        src_ref=follow_src, dst_ref=following, send_sem=tm_send.at[0], recv_sem=tm_recv.at[0],
        device_id=(lax.max(tm - 1, 0), tile), device_id_type=MESH,
    )
    follow_src[...] = restricted(0, coarse)

    @pl.when(tm > 0)
    def _():
        following_copy.start()

    loads[2].wait()
    for at, part in enumerate(parts(coarse_v[...])):
        here = slice(at * coarse, (at + 1) * coarse)
        coarse_own[here, :] = part[:, rim:rim + coarse]
        coarse_rims[here, :] = jnp.concatenate([part[:, :rim], part[:, rim + coarse:]], axis=1)

    @pl.when(first)
    def _():
        state[...] = jnp.zeros(state.shape, F32)
        image[...] = coarse_part(coarse_own, 1, 2) + coarse_part(coarse_rims, 0, 3)

    @pl.loop(0, rows // size)
    def _(j):
        here = pl.ds(pl.multiple_of(j * size, size), size)
        lane = jnp.broadcast_to(map_v[here].reshape(1, size).astype(F32), (size, size))
        column = jnp.transpose(lane).astype(jnp.int32)
        for g in range(coarse // size):
            want = lax.broadcasted_iota(jnp.int32, (size, size), 1) + g * size
            spread_m[here, g * size:(g + 1) * size] = jnp.where(column == want, 1.0, 0.0).astype(BF16)

    take_halo(STEPS - 1)

    @pl.loop(0, blocks)
    def _(b):
        new = row_block(STEPS - 1, b)
        here = pl.ds(pl.multiple_of(b * size, size), size)
        fine[here, :] = new
        fine_2[here, :] = beside(new)

    @pl.when(tm < slices - 1)
    def _():
        following_copy.wait_recv()

    following_tile = lax.min(tm + 1, slices - 1)
    share = rim // CHUNKS
    order = [(half, chunk) for half in (1, 0) for chunk in range(CHUNKS)]
    state_copies, rim_copies = {}, {}
    for at, (half, chunk) in enumerate(order):
        piece = pl.ds(chunk * share, share)
        state_copies[half, chunk] = pltpu.make_async_remote_copy(
            src_ref=sent.at[half, piece], dst_ref=state.at[1 + half, piece], send_sem=tm_send.at[1 + at],
            recv_sem=tm_recv.at[1 + at], device_id=(following_tile, tile), device_id_type=MESH,
        )
        rim_copies[half, chunk] = pltpu.make_async_remote_copy(
            src_ref=state.at[1 + half, piece], dst_ref=state.at[3 if half == 0 else 0, piece],
            send_sem=tm_send.at[1 + 2 * CHUNKS + at], recv_sem=tm_recv.at[1 + 2 * CHUNKS + at],
            device_id=(tm, left if half == 0 else right), device_id_type=MESH,
        )

    def send_state(half):
        span = slice(half * rim, (half + 1) * rim)
        sent[half] = image[span, :] + jump[span, :]
        for chunk in range(CHUNKS):
            state_copies[half, chunk].start()

    for half in (1, 0):
        span = slice(half * rim, (half + 1) * rim)
        jump[span, :] = restricted(half * rim, (half + 1) * rim) - following[span, :]

        @pl.when(first)
        def _():
            send_state(half)

    @pl.when(tm > 0)
    def _():
        for at in order:
            state_copies[at].wait_recv()
            rim_copies[at].start()
        image[...] = coarse_part(coarse_own, 1, 2)
        for at in order:
            rim_copies[at].wait_recv()
        image[...] += coarse_part(coarse_rims, 0, 3)

        @pl.when(tm < slices - 1)
        def _():
            for half in (1, 0):
                send_state(half)

    pair = beside(image[...])
    both = dot(spread_m[...], pair)
    out[...] = fine[...] + (both[:, :tracers] + both[:, tracers:])

    for exchange in exchanges:
        for copy in exchange:
            copy.wait_send()

    @pl.when(tm > 0)
    def _():
        following_copy.wait_send()
        for copy in rim_copies.values():
            copy.wait_send()

    @pl.when(tm < slices - 1)
    def _():
        for copy in state_copies.values():
            copy.wait_send()


def on_device(starts, sources, fine_ops, col_index, live_count, coarse_op, cell_map):
    rows, tracers = sources.shape
    _, blocks, slots, size, _ = fine_ops.shape
    coarse, wide = coarse_op.shape
    rim = (wide - coarse) // 2
    window = blocks + 2 * HALO // size
    anywhere = pl.BlockSpec(memory_space=pltpu.HBM)
    vmem = pl.BlockSpec(memory_space=pltpu.VMEM)
    dma = pltpu.SemaphoreType.DMA
    result = pl.pallas_call(
        kernel,
        out_shape=pltpu.VMEM((rows, tracers), F32),
        in_specs=[anywhere] * 7,
        out_specs=vmem,
        scratch_shapes=[
            pltpu.VMEM((rows,), jnp.int32),
            pltpu.SMEM((slots, blocks), jnp.int32),
            pltpu.SMEM((1, blocks), jnp.int32),
            pltpu.VMEM((rows, tracers), F32),
            pltpu.VMEM((rows, tracers), F32),
            pltpu.VMEM((blocks, slots, size, size), F32),
            pltpu.VMEM((coarse, wide), F32),
            pltpu.VMEM((blocks, 2 * size, slots * size), BF16),
            pltpu.VMEM((2 * coarse, coarse), BF16),
            pltpu.VMEM((2 * coarse, 2 * rim), BF16),
            pltpu.VMEM((STEPS, window, size, 2 * tracers), BF16),
            pltpu.VMEM((STEPS - 1, 2, HALO, tracers), F32),
            pltpu.VMEM((STEPS, 2, HALO, tracers), F32),
            pltpu.VMEM((coarse, rows), BF16),
            pltpu.VMEM((rows, coarse), BF16),
            pltpu.VMEM((coarse, tracers), F32),
            pltpu.VMEM((rows, tracers), F32),
            pltpu.VMEM((rows, 2 * tracers), BF16),
            pltpu.VMEM((coarse, tracers), F32),
            pltpu.VMEM((coarse, tracers), F32),
            pltpu.VMEM((coarse, tracers), F32),
            pltpu.VMEM((2, rim, tracers), F32),
            pltpu.VMEM((4, rim, tracers), F32),
            pltpu.VMEM((coarse, tracers), F32),
            dma((6,)),
            dma((blocks,)),
            dma((STEPS, 2)),
            dma((STEPS, 2)),
            dma((1 + 4 * CHUNKS,)),
            dma((1 + 4 * CHUNKS,)),
        ],
        compiler_params=pltpu.CompilerParams(
            collective_id=0, has_side_effects=True, vmem_limit_bytes=56 * 2**20
        ),
    )(
        starts[0], sources, fine_ops[0], coarse_op, cell_map, col_index[0].T, live_count,
    )
    return result[None]


def solution(mesh):
    placed = (
        P("tm", "tile", None),
        P("tile", None),
        P("tm", "tile", None, None, None),
        P("tm", "tile", None),
        P("tm", "tile"),
        P("tile", None),
        P("tile"),
    )
    return jax.shard_map(
        on_device, mesh=mesh, in_specs=placed, out_specs=P("tm", "tile", None), check_vma=False
    )
```

```python
import jax
import jax.numpy as jnp
from jax import lax
from jax.experimental import pallas as pl
from jax.experimental.pallas import tpu as pltpu
from jax.sharding import PartitionSpec as P

MESH = pl.DeviceIdType.MESH
HALO = 256
STEPS = 2
CHUNKS = 4
F32, BF16 = jnp.float32, jnp.bfloat16


def parts(x):
    high = x.astype(BF16)
    return high, (x - high.astype(F32)).astype(BF16)


def beside(x):
    return jnp.concatenate(parts(x), axis=1)


def dot(a, b):
    return jnp.dot(a, b, preferred_element_type=F32)


def kernel(
    starts, sources, ops, coarse_op, map_hbm, cols_hbm, live_hbm, out,
    map_v, cols, live, start_v, source_v, ops_v, coarse_v, ops_2, coarse_own, coarse_rims, win, edge, halo,
    gather_m, spread_m, inverse, fine, fine_2, following, follow_src, jump, sent, state, image,
    load_sem, ops_sem, halo_send, halo_recv, tm_send, tm_recv,
):
    tm, tile = lax.axis_index("tm"), lax.axis_index("tile")
    slices, tiles = lax.axis_size("tm"), lax.axis_size("tile")
    right, left = lax.rem(tile + 1, tiles), lax.rem(tile + tiles - 1, tiles)
    rows, tracers = starts.shape
    blocks, slots, size, _ = ops.shape
    coarse = coarse_op.shape[0]
    rim = state.shape[1]
    rim_blocks = HALO // size
    first, last = tm == 0, tm == slices - 1

    loads = [
        pltpu.make_async_copy(starts, start_v, load_sem.at[0]),
        pltpu.make_async_copy(sources, source_v, load_sem.at[1]),
        pltpu.make_async_copy(coarse_op, coarse_v, load_sem.at[2]),
        pltpu.make_async_copy(live_hbm, live, load_sem.at[3]),
        pltpu.make_async_copy(cols_hbm, cols, load_sem.at[4]),
        pltpu.make_async_copy(map_hbm, map_v, load_sem.at[5]),
    ]
    for at in (0, 3, 4, 5):
        loads[at].start()

    def ops_load(b):
        return pltpu.make_async_copy(ops.at[b], ops_v.at[b], ops_sem.at[b])

    barrier = pltpu.get_barrier_semaphore()
    for other in (left, right):
        pl.semaphore_signal(barrier, inc=1, device_id=(tm, other), device_id_type=MESH)

    @pl.when(tm > 0)
    def _():
        pl.semaphore_signal(barrier, inc=1, device_id=(tm - 1, tile), device_id_type=MESH)

    @pl.when(tm < slices - 1)
    def _():
        pl.semaphore_signal(barrier, inc=1, device_id=(tm + 1, tile), device_id_type=MESH)

    @pl.loop(0, blocks)
    def _(b):
        ops_load(b).start()

    loads[1].start()
    loads[2].start()
    expected = 2 + jnp.where(first, 0, 1) + jnp.where(last, 0, 1)
    pl.semaphore_wait(barrier, expected)

    def halo_copies(step):
        if step == 0:
            head, tail = starts.at[pl.ds(0, HALO)], starts.at[pl.ds(rows - HALO, HALO)]
        else:
            head, tail = edge.at[step - 1, 0], edge.at[step - 1, 1]
        return [
            pltpu.make_async_remote_copy(
                src_ref=src, dst_ref=halo.at[step, side], send_sem=halo_send.at[step, side],
                recv_sem=halo_recv.at[step, side], device_id=(tm, to), device_id_type=MESH,
            )
            for side, src, to in ((0, tail, right), (1, head, left))
        ]

    exchanges = [halo_copies(step) for step in range(STEPS)]
    for copy in exchanges[0]:
        copy.start()

    def restricted(low, high):
        both = dot(gather_m[low:high, :], fine_2[...])
        return (both[:, :tracers] + both[:, tracers:]) * inverse[low:high, :]

    loads[0].wait()

    @pl.loop(0, blocks)
    def _(b):
        here = pl.ds(pl.multiple_of(b * size, size), size)
        pair = beside(start_v[here, :])
        win[0, b + rim_blocks] = pair
        fine_2[here, :] = pair

    loads[3].wait()

    @pl.loop(0, blocks)
    def _(b):
        ops_load(b).wait()
        for k in range(slots):
            kept = jnp.where(k < live[0, b], 1.0, 0.0)
            high, low = parts(ops_v[b, k] * kept)
            ops_2[b, 0:size, k * size:(k + 1) * size] = high
            ops_2[b, size:2 * size, k * size:(k + 1) * size] = low

    loads[1].wait()
    loads[4].wait()
    loads[5].wait()

    def take_halo(step):
        for side, copy in enumerate(exchanges[step]):
            copy.wait_recv()
            at = 0 if side == 0 else rim_blocks + blocks
            for i in range(rim_blocks):
                win[step, at + i] = beside(halo[step, side, i * size:(i + 1) * size, :])

    def row_block(step, b):
        pieces = jnp.concatenate([win[step, cols[k, b]] for k in range(slots)], axis=0)
        four = dot(ops_2[b], pieces)
        moved = four[:size, :tracers] + (four[:size, tracers:] + four[size:, :tracers])
        return moved + source_v[pl.ds(pl.multiple_of(b * size, size), size), :]

    def coarse_part(operator, low, high):
        held = beside(jnp.concatenate([state[low], state[high]], axis=0))
        four = dot(operator[...], held)
        return four[:coarse, :tracers] + (four[:coarse, tracers:] + four[coarse:, :tracers])

    hits = lax.broadcasted_iota(jnp.int32, (coarse, rows), 0) == map_v[...].reshape(1, rows)
    ones = jnp.where(hits, 1.0, 0.0)
    gather_m[...] = ones.astype(BF16)
    inverse[...] = jnp.broadcast_to(1.0 / jnp.sum(ones, axis=1, keepdims=True), (coarse, tracers))

    following_copy = pltpu.make_async_remote_copy(
        src_ref=follow_src, dst_ref=following, send_sem=tm_send.at[0], recv_sem=tm_recv.at[0],
        device_id=(lax.max(tm - 1, 0), tile), device_id_type=MESH,
    )
    follow_src[...] = restricted(0, coarse)

    @pl.when(tm > 0)
    def _():
        following_copy.start()

    loads[2].wait()
    for at, part in enumerate(parts(coarse_v[...])):
        here = slice(at * coarse, (at + 1) * coarse)
        coarse_own[here, :] = part[:, rim:rim + coarse]
        coarse_rims[here, :] = jnp.concatenate([part[:, :rim], part[:, rim + coarse:]], axis=1)

    @pl.when(first)
    def _():
        state[...] = jnp.zeros(state.shape, F32)
        image[...] = coarse_part(coarse_own, 1, 2) + coarse_part(coarse_rims, 0, 3)

    @pl.loop(0, rows // size)
    def _(j):
        here = pl.ds(pl.multiple_of(j * size, size), size)
        lane = jnp.broadcast_to(map_v[here].reshape(1, size).astype(F32), (size, size))
        column = jnp.transpose(lane).astype(jnp.int32)
        for g in range(coarse // size):
            want = lax.broadcasted_iota(jnp.int32, (size, size), 1) + g * size
            spread_m[here, g * size:(g + 1) * size] = jnp.where(column == want, 1.0, 0.0).astype(BF16)

    for step in range(STEPS - 1):
        take_halo(step)

        def edge_block(side, i):
            b = i if side == 0 else blocks - rim_blocks + i
            new = row_block(step, b)
            edge[step, side, i * size:(i + 1) * size, :] = new
            win[step + 1, b + rim_blocks] = beside(new)

        for side in (0, 1):
            for i in range(rim_blocks):
                edge_block(side, i)
            exchanges[step + 1][1 - side].start()

        @pl.loop(rim_blocks, blocks - rim_blocks)
        def _(b):
            win[step + 1, b + rim_blocks] = beside(row_block(step, b))

    take_halo(STEPS - 1)

    @pl.loop(0, blocks)
    def _(b):
        new = row_block(STEPS - 1, b)
        here = pl.ds(pl.multiple_of(b * size, size), size)
        fine[here, :] = new
        fine_2[here, :] = beside(new)

    @pl.when(tm < slices - 1)
    def _():
        following_copy.wait_recv()

    following_tile = lax.min(tm + 1, slices - 1)
    share = rim // CHUNKS
    order = [(half, chunk) for half in (1, 0) for chunk in range(CHUNKS)]
    state_copies, rim_copies = {}, {}
    for at, (half, chunk) in enumerate(order):
        piece = pl.ds(chunk * share, share)
        state_copies[half, chunk] = pltpu.make_async_remote_copy(
            src_ref=sent.at[half, piece], dst_ref=state.at[1 + half, piece], send_sem=tm_send.at[1 + at],
            recv_sem=tm_recv.at[1 + at], device_id=(following_tile, tile), device_id_type=MESH,
        )
        rim_copies[half, chunk] = pltpu.make_async_remote_copy(
            src_ref=state.at[1 + half, piece], dst_ref=state.at[3 if half == 0 else 0, piece],
            send_sem=tm_send.at[1 + 2 * CHUNKS + at], recv_sem=tm_recv.at[1 + 2 * CHUNKS + at],
            device_id=(tm, left if half == 0 else right), device_id_type=MESH,
        )

    def send_state(half):
        span = slice(half * rim, (half + 1) * rim)
        sent[half] = image[span, :] + jump[span, :]
        for chunk in range(CHUNKS):
            state_copies[half, chunk].start()

    for half in (1, 0):
        span = slice(half * rim, (half + 1) * rim)
        jump[span, :] = restricted(half * rim, (half + 1) * rim) - following[span, :]

        @pl.when(first)
        def _():
            send_state(half)

    @pl.when(tm > 0)
    def _():
        for at in order:
            state_copies[at].wait_recv()
            rim_copies[at].start()
        image[...] = coarse_part(coarse_own, 1, 2)
        for at in order:
            rim_copies[at].wait_recv()
        image[...] += coarse_part(coarse_rims, 0, 3)

        @pl.when(tm < slices - 1)
        def _():
            for half in (1, 0):
                send_state(half)

    pair = beside(image[...])
    both = dot(spread_m[...], pair)
    out[...] = fine[...] + (both[:, :tracers] + both[:, tracers:])

    for exchange in exchanges:
        for copy in exchange:
            copy.wait_send()

    @pl.when(tm > 0)
    def _():
        following_copy.wait_send()
        for copy in rim_copies.values():
            copy.wait_send()

    @pl.when(tm < slices - 1)
    def _():
        for copy in state_copies.values():
            copy.wait_send()


def on_device(starts, sources, fine_ops, col_index, live_count, coarse_op, cell_map):
    rows, tracers = sources.shape
    _, blocks, slots, size, _ = fine_ops.shape
    coarse, wide = coarse_op.shape
    rim = (wide - coarse) // 2
    window = blocks + 2 * HALO // size
    anywhere = pl.BlockSpec(memory_space=pltpu.HBM)
    vmem = pl.BlockSpec(memory_space=pltpu.VMEM)
    dma = pltpu.SemaphoreType.DMA
    result = pl.pallas_call(
        kernel,
        out_shape=pltpu.VMEM((rows, tracers), F32),
        in_specs=[anywhere] * 7,
        out_specs=vmem,
        scratch_shapes=[
            pltpu.VMEM((rows,), jnp.int32),
            pltpu.SMEM((slots, blocks), jnp.int32),
            pltpu.SMEM((1, blocks), jnp.int32),
            pltpu.VMEM((rows, tracers), F32),
            pltpu.VMEM((rows, tracers), F32),
            pltpu.VMEM((blocks, slots, size, size), F32),
            pltpu.VMEM((coarse, wide), F32),
            pltpu.VMEM((blocks, 2 * size, slots * size), BF16),
            pltpu.VMEM((2 * coarse, coarse), BF16),
            pltpu.VMEM((2 * coarse, 2 * rim), BF16),
            pltpu.VMEM((STEPS, window, size, 2 * tracers), BF16),
            pltpu.VMEM((STEPS - 1, 2, HALO, tracers), F32),
            pltpu.VMEM((STEPS, 2, HALO, tracers), F32),
            pltpu.VMEM((coarse, rows), BF16),
            pltpu.VMEM((rows, coarse), BF16),
            pltpu.VMEM((coarse, tracers), F32),
            pltpu.VMEM((rows, tracers), F32),
            pltpu.VMEM((rows, 2 * tracers), BF16),
            pltpu.VMEM((coarse, tracers), F32),
            pltpu.VMEM((coarse, tracers), F32),
            pltpu.VMEM((coarse, tracers), F32),
            pltpu.VMEM((2, rim, tracers), F32),
            pltpu.VMEM((4, rim, tracers), F32),
            pltpu.VMEM((coarse, tracers), F32),
            dma((6,)),
            dma((blocks,)),
            dma((STEPS, 2)),
            dma((STEPS, 2)),
            dma((1 + 4 * CHUNKS,)),
            dma((1 + 4 * CHUNKS,)),
        ],
        compiler_params=pltpu.CompilerParams(
            collective_id=0, has_side_effects=True, vmem_limit_bytes=56 * 2**20
        ),
    )(
        starts[0], sources, fine_ops[0], coarse_op, cell_map, col_index[0].T, live_count,
    )
    return result[None]


def solution(mesh):
    placed = (
        P("tm", "tile", None),
        P("tile", None),
        P("tm", "tile", None, None, None),
        P("tm", "tile", None),
        P("tm", "tile"),
        P("tile", None),
        P("tile"),
    )
    return jax.shard_map(
        on_device, mesh=mesh, in_specs=placed, out_specs=P("tm", "tile", None), check_vma=False
    )
```
